768 devices in a mesh: batch: 16 (over z_hi, x), feat: 48 (over y, z_lo, core).
Axes of the slice: x: 4, y: 8, z: 12 (z_hi: 4, z_lo: 3; z = z_hi * 3 + z_lo), core: 2. Of those that a mesh axis runs over, the one named last changes fastest.
Arguments:
- view_a: bfloat16 [2048, 6144], P('batch', 'feat'), may hold values from -6 to 6
- view_b: bfloat16 [2048, 6144], P('batch', 'feat'), may hold values from -6 to 6
- weight_off: float32 [], replicated, may hold values from 0.05 to 0.2
- loss_grad: float32 [], replicated, may hold values from 0.5 to 2
Outputs:
- grad_a: float32 [2048, 6144], P('batch', 'feat')
- grad_b: float32 [2048, 6144], P('batch', 'feat')
The draws below stay inside these ranges and needn't reach their ends.
All inputs are finite; a program needn't handle non-finite values.
Results may differ from the reference program's by a relative error of at most 0.0012.
Values may be sent and summed in bfloat16 or wider, within the bound.
A program may use at most 32 MiB of HBM per device.

```python
import math
import jax
import jax.numpy as jnp
from jax import lax

BATCH = 2048
FEATURES = 6144


def common_views(key):
    base = jax.random.normal(jax.random.fold_in(key, 11), (BATCH, FEATURES), jnp.float32)
    other = jax.random.normal(jax.random.fold_in(key, 12), (BATCH, FEATURES), jnp.float32)
    mixing = jax.random.uniform(jax.random.fold_in(key, 13), (1, FEATURES), jnp.float32, 0.2, 0.95)
    return (base, mixing * base + jnp.sqrt(1.0 - mixing * mixing) * other)


def draw_view_a(key, part):
    first, second = common_views(key)
    values = first
    return jnp.clip(values, -6.0, 6.0).astype(jnp.bfloat16)


def draw_view_b(key, part):
    first, second = common_views(key)
    values = second
    return jnp.clip(values, -6.0, 6.0).astype(jnp.bfloat16)


def setup_inputs(seed: int = 0) -> dict:
    key_list = jax.random.split(jax.random.key(seed), 5)
    return {
        "view_a": draw_view_a(jax.random.fold_in(key_list[4], 71), 0),
        "view_b": draw_view_b(jax.random.fold_in(key_list[4], 71), 0),
        "weight_off": jnp.clip(jnp.exp(jax.random.uniform(key_list[2], (), jnp.float32, math.log(0.05), math.log(0.2))), 0.05, 0.2),
        "loss_grad": jnp.clip(jax.random.uniform(key_list[3], (), jnp.float32, 0.5, 2.0), 0.5, 2.0),
    }


def reference(view_a, view_b, weight_off, loss_grad):
    corr = lax.dot_general(view_a, view_b, (((0,), (0,)), ((), ())), preferred_element_type=jnp.float32) / BATCH
    diagonal_mask = jnp.eye(FEATURES, dtype=bool)
    weights = jnp.where(diagonal_mask, -2.0 * (1.0 - corr), 2.0 * weight_off * corr)
    first = view_a.astype(jnp.float32)
    second = view_b.astype(jnp.float32)
    grad_a = lax.dot_general(second, weights, (((1,), (1,)), ((), ())), precision=lax.Precision.HIGHEST, preferred_element_type=jnp.float32)
    grad_b = jnp.dot(first, weights, precision=lax.Precision.HIGHEST, preferred_element_type=jnp.float32)
    return loss_grad * grad_a, loss_grad * grad_b
```

```python
import jax
import jax.numpy as jnp
from jax import lax
from jax.sharding import PartitionSpec as P


def local(view_a, view_b, weight_off, loss_grad):
    rows, width = view_a.shape
    images = rows * lax.axis_size("batch")
    own = jnp.stack([view_a, view_b])
    cols = lax.all_gather(own, "batch", axis=1, tiled=True)
    gram_part = lax.dot_general(
        own, cols, (((2,), (2,)), ((0,), (0,))), preferred_element_type=jnp.float32
    )
    gram = lax.psum(gram_part, "feat")
    diag = jnp.sum(cols[0].astype(jnp.float32) * cols[1].astype(jnp.float32), axis=0) / images
    shift = -2.0 + 2.0 * (1.0 - weight_off) * diag
    rounded = lax.reduce_precision(gram, 8, 7)
    high = rounded.astype(jnp.bfloat16)
    low = (gram - rounded).astype(jnp.bfloat16)

    def apply(which, other):
        out = jnp.dot(high[which], cols[other], preferred_element_type=jnp.float32)
        return out + jnp.dot(low[which], cols[other], preferred_element_type=jnp.float32)

    scale = 2.0 * weight_off / images
    grad_a = loss_grad * (scale * apply(1, 0) + view_b.astype(jnp.float32) * shift)
    grad_b = loss_grad * (scale * apply(0, 1) + view_a.astype(jnp.float32) * shift)
    return grad_a, grad_b


def solution(mesh):
    return jax.shard_map(
        local,
        mesh=mesh,
        in_specs=(P("batch", "feat"), P("batch", "feat"), P(), P()),
        out_specs=(P("batch", "feat"), P("batch", "feat")),
        check_vma=False,
    )
```

```python
import functools

import jax
import jax.numpy as jnp
from jax import lax
from jax.experimental import pallas as pl
from jax.experimental.pallas import tpu as pltpu
from jax.sharding import PartitionSpec as P

MESH = pl.DeviceIdType.MESH
NX, NY, NHI, NLO = 4, 8, 4, 3
NZ = NHI * NLO
T = 128
J = 48
JR = NX * J
PY = JR // NY
HOPS = ((6, 5), (5, 6))


def dev(x, y, z, c):
    return ((z // NLO) * NX + x, (y * NLO + z % NLO) * 2 + c)


def kernel(
    images,
    w_ref,
    l_ref,
    a_ref,
    b_ref,
    ga_ref,
    gb_ref,
    own,
    xbuf,
    xj,
    part,
    rsb,
    red,
    gt,
    op,
    rx,
    fsum,
    fin,
    dgs,
    dgx,
    dgs2,
    dgz,
    ssem,
    p1r,
    sibr,
    p2r,
    rsr,
    agr,
    p4r,
    p5r,
    dxr,
    dzr,
):
    bi = lax.axis_index("batch")
    fi = lax.axis_index("feat")
    zh, x = bi // NX, bi % NX
    y, zl, c = fi // (NLO * 2), (fi // 2) % NLO, fi % 2
    z = zh * NLO + zl
    zr, zf = (z + 1) % NZ, (z + NZ - 1) % NZ

    def at_z(k):
        return (z + k + 2 * NZ) % NZ

    peers = [dev(x, y, zn, t) for zn in (zr, zf) for t in range(2)]
    peers += [dev(x, y, z, 1 - c)]
    peers += [dev((x + d) % NX, y, z, c) for d in range(1, NX)]
    peers += [dev(x, (y + d) % NY, z, t) for d in range(1, NY) for t in range(2)]
    peers += [dev(x, y, zh * NLO + (zl + d) % NLO, t) for d in range(1, NLO) for t in range(2)]
    peers += [dev(x, y, (z + NLO * d) % NZ, c) for d in range(1, NHI)]
    bar = pltpu.get_barrier_semaphore()
    for p in peers:
        pl.semaphore_signal(bar, inc=1, device_id=p, device_id_type=MESH)
    own[0] = a_ref[...]
    own[1] = b_ref[...]
    prod = a_ref[...].astype(jnp.float32) * b_ref[...].astype(jnp.float32)
    dgs[...] = jnp.sum(prod.reshape(T // 8, 8, T), axis=0)
    xbuf[z, c] = own[c]
    pl.semaphore_wait(bar, len(peers))

    sent = []

    def copy(src, dst, rsem, target):
        cp = pltpu.make_async_remote_copy(
            src_ref=src,
            dst_ref=dst,
            send_sem=ssem.at[len(sent)],
            recv_sem=rsem,
            device_id=target,
            device_id_type=MESH,
        )
        sent.append(cp)
        cp.start()

    def arrived(dst, rsem):
        pltpu.make_async_remote_copy(
            src_ref=dst,
            dst_ref=dst,
            send_sem=ssem.at[0],
            recv_sem=rsem,
            device_id=dev(x, y, z, 1 - c),
            device_id_type=MESH,
        ).wait_recv()

    for t in range(2):
        copy(own.at[t], xbuf.at[z, c], p1r.at[0, 0, c], dev(x, y, zr, t))
        copy(own.at[t], xbuf.at[z, c], p1r.at[1, 0, c], dev(x, y, zf, t))
    copy(own.at[1 - c], xbuf.at[z, c], sibr.at[0], dev(x, y, z, 1 - c))
    for d in range(1, NX):
        copy(dgs, dgx.at[d - 1], dxr.at[d - 1], dev((x + d) % NX, y, z, c))

    near = jnp.where(zl == 2, 1, NHI - 1)
    group = [zh, (zh + near) % NHI, (zh + NHI - near) % NHI, (zh + 2) % NHI]
    first = jnp.where(zl == 2, T - J, zl * J)
    first = pl.multiple_of(first, 16)

    def send_j():
        xj[:, :, x] = xbuf[pl.ds(zh * NLO, NLO), :, pl.ds(first, J), :]
        for d in (2, 1, 3):
            x1 = (x + d) % NX
            copy(
                xbuf.at[pl.ds(zh * NLO, NLO), :, pl.ds(first, J), :],
                xj.at[:, :, x],
                p2r.at[d - 1],
                dev(x1, y, z, c),
            )

    def wait_j():
        for d in (1, 3, 2):
            arrived(xj.at[:, :, (x + NX - d) % NX], p2r.at[d - 1])

    def gram(k):
        acc = jnp.zeros((JR, T), jnp.float32)
        for i in range(NLO):
            for j in range(2):
                acc += lax.dot_general(
                    xj[i, j].reshape(JR, T),
                    xbuf[group[k] * NLO + i, j],
                    (((1,), (1,)), ((), ())),
                    preferred_element_type=jnp.float32,
                )
        part[k] = acc
        for d in (4, 3, 5, 2, 6, 1, 7):
            y1 = (y + d) % NY
            copy(
                part.at[k, pl.ds(pl.multiple_of(y1 * PY, 8), PY), :],
                rsb.at[k, d - 1],
                rsr.at[k, d - 1],
                dev(x, y1, z, c),
            )

    def reduce(k):
        tot = part[k, pl.ds(pl.multiple_of(y * PY, 8), PY), :]
        for d in (1, 7, 2, 6, 3, 5, 4):
            arrived(rsb.at[k, d - 1], rsr.at[k, d - 1])
            tot += rsb[k, d - 1]
        red[k] = tot
        for d in (4, 3, 5, 2, 6, 1, 7, 0):
            copy(
                red.at[k],
                gt.at[k, pl.ds(pl.multiple_of(y * PY, 8), PY), :],
                agr.at[k, d],
                dev(x, (y + d) % NY, z, 1 - c),
            )

    for s in range(6):
        for j in range(2):
            for r in range(2):
                if s >= HOPS[r][j]:
                    continue
                zc = at_z(-1 - s) if r == 0 else at_z(1 + s)
                arrived(xbuf.at[zc, j], p1r.at[r, s, j])
                if s + 1 < HOPS[r][j]:
                    copy(
                        xbuf.at[zc, j],
                        xbuf.at[zc, j],
                        p1r.at[r, s + 1, j],
                        dev(x, y, zr if r == 0 else zf, c),
                    )
        if s == 0:
            arrived(xbuf.at[z, 1 - c], sibr.at[0])
        if s == 1:
            send_j()
        if s == 2:
            tot = dgs[...]
            for d in range(1, NX):
                arrived(dgx.at[d - 1], dxr.at[d - 1])
                tot += dgx[d - 1]
            dgs2[...] = tot
            for d in range(1, NHI):
                copy(dgs2, dgz.at[d - 1], dzr.at[d - 1], dev(x, y, (z + NLO * d) % NZ, c))
            wait_j()
            gram(0)
        if s == 3:
            gram(1)
        if s == 4:
            gram(2)
            reduce(0)
    gram(3)
    reduce(1)
    reduce(2)
    reduce(3)

    for k in range(NHI):
        for d in range(NY):
            y1 = (y + NY - d) % NY
            arrived(gt.at[k, pl.ds(pl.multiple_of(y1 * PY, 8), PY), :], agr.at[k, d])
        g = gt[k]
        high = g.astype(jnp.bfloat16)
        low = (g - high.astype(jnp.float32)).astype(jnp.bfloat16)
        for f in range(NLO * 2):
            tile = xbuf[group[k] * NLO + f // 2, f % 2]
            new = jnp.dot(high, tile, preferred_element_type=jnp.float32)
            new += jnp.dot(low, tile, preferred_element_type=jnp.float32)
            new = new.reshape(NX, J, T)
            op[f] = new if k == 0 else op[f] + new
    for d in (2, 1, 3):
        x1 = (x + d) % NX
        copy(op.at[:, x1], rx.at[d - 1], p4r.at[d - 1], dev(x1, y, z, c))
    total = op[:, x]
    for d in (1, 3, 2):
        arrived(rx.at[d - 1], p4r.at[d - 1])
        total += rx[d - 1]
    fsum[...] = total

    fin[c, zl] = fsum[zl * 2 + c]
    hops = [(d, e) for d in range(NLO) for e in range(2) if d or e]
    for d, e in hops:
        zl1, c1 = (zl + d) % NLO, (c + e) % 2
        copy(fsum.at[zl1 * 2 + c1], fin.at[c, zl], p5r.at[d, e], dev(x, y, zh * NLO + zl1, c1))
    tot = dgs2[...]
    for d in range(1, NHI):
        arrived(dgz.at[d - 1], dzr.at[d - 1])
        tot += dgz[d - 1]
    weight_off = w_ref[0]
    loss_grad = l_ref[0]
    shift = -2.0 + (2.0 * (1.0 - weight_off) / images) * jnp.sum(tot, axis=0, keepdims=True)
    scale = 2.0 * weight_off / images
    for d, e in hops:
        arrived(fin.at[(c + e) % 2, (zl + NLO - d) % NLO], p5r.at[d, e])
    for t, (out, other) in enumerate(((ga_ref, b_ref), (gb_ref, a_ref))):
        for i, rows in enumerate((J, J, T - 2 * J)):
            at = pl.ds(i * J, rows)
            gram_term = fin[t, i, pl.ds(J - rows, rows), :]
            out[at, :] = loss_grad * (scale * gram_term + other[at, :].astype(jnp.float32) * shift)
    for cp in sent:
        cp.wait_send()


def local(view_a, view_b, weight_off, loss_grad):
    images = view_a.shape[0] * lax.axis_size("batch")
    f32, bf16 = jnp.float32, jnp.bfloat16
    dma = pltpu.SemaphoreType.DMA
    vmem = pl.BlockSpec(memory_space=pltpu.VMEM)
    smem = pl.BlockSpec(memory_space=pltpu.SMEM)
    return pl.pallas_call(
        functools.partial(kernel, float(images)),
        out_shape=[jax.ShapeDtypeStruct((T, T), f32)] * 2,
        in_specs=[smem, smem, vmem, vmem],
        out_specs=[vmem, vmem],
        scratch_shapes=[
            pltpu.VMEM((2, T, T), bf16),
            pltpu.VMEM((NZ, 2, T, T), bf16),
            pltpu.VMEM((NLO, 2, NX, J, T), bf16),
            pltpu.VMEM((NHI, JR, T), f32),
            pltpu.VMEM((NHI, NY - 1, PY, T), f32),
            pltpu.VMEM((NHI, PY, T), f32),
            pltpu.VMEM((NHI, JR, T), f32),
            pltpu.VMEM((NLO * 2, NX, J, T), f32),
            pltpu.VMEM((NX - 1, NLO * 2, J, T), f32),
            pltpu.VMEM((NLO * 2, J, T), f32),
            pltpu.VMEM((2, NLO, J, T), f32),
            pltpu.VMEM((8, T), f32),
            pltpu.VMEM((NX - 1, 8, T), f32),
            pltpu.VMEM((8, T), f32),
            pltpu.VMEM((NHI - 1, 8, T), f32),
            dma((104,)),
            dma((2, 6, 2)),
            dma((1,)),
            dma((NX - 1,)),
            dma((NHI, NY - 1)),
            dma((NHI, NY)),
            dma((NX - 1,)),
            dma((NLO, 2)),
            dma((NX - 1,)),
            dma((NHI - 1,)),
        ],
        compiler_params=pltpu.CompilerParams(
            collective_id=0, has_side_effects=True, vmem_limit_bytes=32 << 20
        ),
        name="gram_grads",
    )(weight_off.reshape(1), loss_grad.reshape(1), view_a, view_b)


def solution(mesh):
    return jax.shard_map(
        local,
        mesh=mesh,
        in_specs=(P("batch", "feat"), P("batch", "feat"), P(), P()),
        out_specs=(P("batch", "feat"), P("batch", "feat")),
        check_vma=False,
    )
```

```python
import functools

import jax
import jax.numpy as jnp
from jax import lax
from jax.experimental import pallas as pl
from jax.experimental.pallas import tpu as pltpu
from jax.sharding import PartitionSpec as P

MESH = pl.DeviceIdType.MESH
NX, NY, NHI, NLO = 4, 8, 4, 3
NZ = NHI * NLO
T = 128
J = 48
JR = NX * J
PY = JR // NY
TREE = {2: 0, -2: 0, 1: 0, -1: 0, 4: 2, -4: -2, 3: 2, -3: -2, 5: 4, -5: -4, 6: 4}
NEXT = {p: [d for d in TREE if TREE[d] == p] for p in (0, *TREE)}
FAR = max(abs(d) for d in NEXT[0])


def dev(x, y, z, c):
    return ((z // NLO) * NX + x, (y * NLO + z % NLO) * 2 + c)


def kernel(
    images,
    w_ref,
    l_ref,
    a_ref,
    b_ref,
    ga_ref,
    gb_ref,
    own,
    xbuf,
    xj,
    part,
    rsb,
    red,
    gt,
    op,
    rx,
    fsum,
    fin,
    dgs,
    dgx,
    dgs2,
    dgz,
    ssem,
    loaded,
    xin,
    yin,
    p1r,
    sibr,
    p2r,
    rsr,
    agr,
    p4r,
    p5r,
    dxr,
    dzr,
):
    bi = lax.axis_index("batch")
    fi = lax.axis_index("feat")
    zh, x = bi // NX, bi % NX
    y, zl, c = fi // (NLO * 2), (fi // 2) % NLO, fi % 2
    z = zh * NLO + zl

    def at_z(k):
        return (z + k + 2 * NZ) % NZ

    yr, yl = (y + 1) % NY, (y + NY - 1) % NY
    xr, xl = (x + 1) % NX, (x + NX - 1) % NX
    bar = pltpu.get_barrier_semaphore()
    peers = [dev(x, y, z, 1 - c)]
    peers += [dev(x, yn, z, t) for yn in (yr, yl) for t in range(2)]
    peers += [dev(xn, y, z, c) for xn in (xr, xl)]
    peers += [dev(x, y, at_z(s * d), t) for d in range(1, FAR + 1) for s in (1, -1) for t in range(2)]
    for p in peers:
        pl.semaphore_signal(bar, inc=1, device_id=p, device_id_type=MESH)
    loads = [
        pltpu.make_async_copy(ref, own.at[t], loaded.at[t]) for t, ref in enumerate((a_ref, b_ref))
    ]
    for cp in loads:
        cp.start()
    for cp in loads:
        cp.wait()
    xbuf[z, c] = own[c]
    pl.semaphore_wait(bar, len(peers))

    sent = []

    def copy(src, dst, rsem, target):
        cp = pltpu.make_async_remote_copy(
            src_ref=src,
            dst_ref=dst,
            send_sem=ssem.at[len(sent)],
            recv_sem=rsem,
            device_id=target,
            device_id_type=MESH,
        )
        sent.append(cp)
        cp.start()

    def arrived(dst, rsem):
        pltpu.make_async_remote_copy(
            src_ref=dst,
            dst_ref=dst,
            send_sem=ssem.at[0],
            recv_sem=rsem,
            device_id=dev(x, y, z, 1 - c),
            device_id_type=MESH,
        ).wait_recv()

    sign = 1 - 2 * c
    for t in range(2):
        for d in NEXT[0]:
            copy(own.at[t], xbuf.at[z, c], p1r.at[c, d + 5], dev(x, y, at_z(sign * d), t))
        if t == 0:
            pl.semaphore_signal(xin, inc=1, device_id=dev(xl, y, z, c), device_id_type=MESH)
            copy(own.at[1 - c], xbuf.at[z, c], sibr.at[0], dev(x, y, z, 1 - c))
    for n in range(NY // 2 - 1):
        for i, yn in enumerate((yr, yl)):
            pl.semaphore_signal(yin.at[n, i], inc=1, device_id=dev(x, yn, z, c), device_id_type=MESH)
        for i in range(2):
            pl.semaphore_wait(yin.at[n, i], 1)
    pl.semaphore_wait(xin, 1)
    first_view, second_view = own[0].astype(jnp.float32), own[1].astype(jnp.float32)
    dgs[...] = jnp.sum((first_view * second_view).reshape(T // 8, 8, T), axis=0)
    for d in range(1, NX):
        copy(dgs, dgx.at[d - 1], dxr.at[d - 1], dev((x + d) % NX, y, z, c))

    near = jnp.where(zl == 2, 1, NHI - 1)
    group = [zh, (zh + near) % NHI, (zh + NHI - near) % NHI, (zh + 2) % NHI]
    first = jnp.where(zl == 2, T - J, zl * J)
    first = pl.multiple_of(first, 16)

    def send_j():
        xj[:, :, x] = xbuf[pl.ds(zh * NLO, NLO), :, pl.ds(first, J), :]
        for d in (2, 1, 3):
            x1 = (x + d) % NX
            copy(
                xbuf.at[pl.ds(zh * NLO, NLO), :, pl.ds(first, J), :],
                xj.at[:, :, x],
                p2r.at[d - 1],
                dev(x1, y, z, c),
            )

    def wait_j():
        for d in (1, 3, 2):
            arrived(xj.at[:, :, (x + NX - d) % NX], p2r.at[d - 1])

    def gram(k):
        acc = jnp.zeros((JR, T), jnp.float32)
        for i in range(NLO):
            for j in range(2):
                acc += lax.dot_general(
                    xj[i, j].reshape(JR, T),
                    xbuf[group[k] * NLO + i, j],
                    (((1,), (1,)), ((), ())),
                    preferred_element_type=jnp.float32,
                )
        part[k] = acc
        for d in (4, 3, 5, 2, 6, 1, 7):
            y1 = (y + d) % NY
            copy(
                part.at[k, pl.ds(pl.multiple_of(y1 * PY, 8), PY), :],
                rsb.at[k, d - 1],
                rsr.at[k, d - 1],
                dev(x, y1, z, c),
            )

    def reduce(k):
        tot = part[k, pl.ds(pl.multiple_of(y * PY, 8), PY), :]
        for d in (1, 7, 2, 6, 3, 5, 4):
            arrived(rsb.at[k, d - 1], rsr.at[k, d - 1])
            tot += rsb[k, d - 1]
        red[k] = tot
        for d in (4, 3, 5, 2, 6, 1, 7, 0):
            copy(
                red.at[k],
                gt.at[k, pl.ds(pl.multiple_of(y * PY, 8), PY), :],
                agr.at[k, d],
                dev(x, (y + d) % NY, z, 1 - c),
            )

    for d in TREE:
        for j in range(2):
            s = 1 - 2 * j
            zc = at_z(-s * d)
            arrived(xbuf.at[zc, j], p1r.at[j, d + 5])
            for e in NEXT[d]:
                copy(xbuf.at[zc, j], xbuf.at[zc, j], p1r.at[j, e + 5], dev(x, y, at_z(s * (e - d)), c))
        if d == -1:
            arrived(xbuf.at[z, 1 - c], sibr.at[0])
            send_j()
        if d == -3:
            wait_j()
            gram(0)
            gram(1)
        if d == -5:
            gram(2)
    gram(3)
    tot = dgs[...]
    for d in range(1, NX):
        arrived(dgx.at[d - 1], dxr.at[d - 1])
        tot += dgx[d - 1]
    dgs2[...] = tot
    for d in range(1, NHI):
        copy(dgs2, dgz.at[d - 1], dzr.at[d - 1], dev(x, y, (z + NLO * d) % NZ, c))
    for k in range(NHI):
        reduce(k)

    for k in range(NHI):
        for d in range(NY):
            y1 = (y + NY - d) % NY
            arrived(gt.at[k, pl.ds(pl.multiple_of(y1 * PY, 8), PY), :], agr.at[k, d])
        g = gt[k]
        high = g.astype(jnp.bfloat16)
        low = (g - high.astype(jnp.float32)).astype(jnp.bfloat16)
        for d in (1, 2, 0):
            zl1 = (zl + d) % NLO
            for e in range(2):
                tile = xbuf[group[k] * NLO + zl1, e]
                new = jnp.dot(high, tile, preferred_element_type=jnp.float32)
                new += jnp.dot(low, tile, preferred_element_type=jnp.float32)
                new = new.reshape(NX, J, T)
                op[d, :, e] = new if k == 0 else op[d, :, e] + new
            if k == NHI - 1:
                for i in (2, 1, 3):
                    x1 = (x + i) % NX
                    copy(op.at[d, x1], rx.at[d, i - 1], p4r.at[d, i - 1], dev(x1, y, z, c))
    for d in (1, 2, 0):
        zl1 = (zl + d) % NLO
        total = op[d, x]
        for i in (1, 3, 2):
            arrived(rx.at[d, i - 1], p4r.at[d, i - 1])
            total += rx[d, i - 1]
        fsum[d] = total
        for e in range(2):
            c1 = (c + e) % 2
            if d or e:
                copy(fsum.at[d, c1], fin.at[c, zl], p5r.at[d, e], dev(x, y, zh * NLO + zl1, c1))
            else:
                fin[c, zl] = fsum[d, c]
    hops = [(d, e) for d in (0, 1, 2) for e in range(2) if d or e]
    tot = dgs2[...]
    for d in range(1, NHI):
        arrived(dgz.at[d - 1], dzr.at[d - 1])
        tot += dgz[d - 1]
    weight_off = w_ref[0]
    loss_grad = l_ref[0]
    shift = -2.0 + (2.0 * (1.0 - weight_off) / images) * jnp.sum(tot, axis=0, keepdims=True)
    scale = 2.0 * weight_off / images
    for d, e in hops:
        arrived(fin.at[(c + e) % 2, (zl + NLO - d) % NLO], p5r.at[d, e])
    for t, (out, other) in enumerate(((ga_ref, own.at[1]), (gb_ref, own.at[0]))):
        for i, rows in enumerate((J, J, T - 2 * J)):
            at = pl.ds(i * J, rows)
            gram_term = fin[t, i, pl.ds(J - rows, rows), :]
            out[at, :] = loss_grad * (scale * gram_term + other[at, :].astype(jnp.float32) * shift)
    for cp in sent:
        cp.wait_send()


def local(view_a, view_b, weight_off, loss_grad):
    images = view_a.shape[0] * lax.axis_size("batch")
    f32, bf16 = jnp.float32, jnp.bfloat16
    dma = pltpu.SemaphoreType.DMA
    vmem = pl.BlockSpec(memory_space=pltpu.VMEM)
    hbm = pl.BlockSpec(memory_space=pl.ANY)
    smem = pl.BlockSpec(memory_space=pltpu.SMEM)
    return pl.pallas_call(
        functools.partial(kernel, float(images)),
        out_shape=[jax.ShapeDtypeStruct((T, T), f32)] * 2,
        in_specs=[smem, smem, hbm, hbm],
        out_specs=[vmem, vmem],
        scratch_shapes=[
            pltpu.VMEM((2, T, T), bf16),
            pltpu.VMEM((NZ, 2, T, T), bf16),
            pltpu.VMEM((NLO, 2, NX, J, T), bf16),
            pltpu.VMEM((NHI, JR, T), f32),
            pltpu.VMEM((NHI, NY - 1, PY, T), f32),
            pltpu.VMEM((NHI, PY, T), f32),
            pltpu.VMEM((NHI, JR, T), f32),
            pltpu.VMEM((NLO, NX, 2, J, T), f32),
            pltpu.VMEM((NLO, NX - 1, 2, J, T), f32),
            pltpu.VMEM((NLO, 2, J, T), f32),
            pltpu.VMEM((2, NLO, J, T), f32),
            pltpu.VMEM((8, T), f32),
            pltpu.VMEM((NX - 1, 8, T), f32),
            pltpu.VMEM((8, T), f32),
            pltpu.VMEM((NHI - 1, 8, T), f32),
            dma((112,)),
            dma((2,)),
            pltpu.SemaphoreType.REGULAR,
            pltpu.SemaphoreType.REGULAR((NY // 2 - 1, 2)),
            dma((2, 12)),
            dma((1,)),
            dma((NX - 1,)),
            dma((NHI, NY - 1)),
            dma((NHI, NY)),
            dma((NLO, NX - 1)),
            dma((NLO, 2)),
            dma((NX - 1,)),
            dma((NHI - 1,)),
        ],
        compiler_params=pltpu.CompilerParams(
            collective_id=0, has_side_effects=True, vmem_limit_bytes=60 << 20
        ),
        name="gram_grads",
    )(weight_off.reshape(1), loss_grad.reshape(1), view_a, view_b)


def solution(mesh):
    return jax.shard_map(
        local,
        mesh=mesh,
        in_specs=(P("batch", "feat"), P("batch", "feat"), P(), P()),
        out_specs=(P("batch", "feat"), P("batch", "feat")),
        check_vma=False,
    )
```

```python
import functools

import jax
import jax.numpy as jnp
from jax import lax
from jax.experimental import pallas as pl
from jax.experimental.pallas import tpu as pltpu
from jax.sharding import PartitionSpec as P

MESH = pl.DeviceIdType.MESH
NX, NY, NHI, NLO = 4, 8, 4, 3
NZ = NHI * NLO
T = 128
J = 48
JR = NX * J
PY = JR // NY
TREE = {2: 0, -2: 0, 1: 0, -1: 0, 4: 2, -4: -2, 3: 2, -3: -2, 5: 4, -5: -4, 6: 4}
NEXT = {p: [d for d in TREE if TREE[d] == p] for p in (0, *TREE)}
FAR = max(abs(d) for d in NEXT[0])


def dev(x, y, z, c):
    return ((z // NLO) * NX + x, (y * NLO + z % NLO) * 2 + c)


def kernel(
    images,
    w_ref,
    a_ref,
    b_ref,
    g_ref,
    own,
    xbuf,
    xj,
    part,
    rsb,
    red,
    gt,
    op,
    rx,
    fsum,
    fin,
    dgs,
    dgx,
    dgs2,
    dgz,
    ssem,
    loaded,
    xin,
    yin,
    p1r,
    sibr,
    p2r,
    rsr,
    agr,
    p4r,
    p5r,
    dxr,
    dzr,
):
    bi = lax.axis_index("batch")
    fi = lax.axis_index("feat")
    zh, x = bi // NX, bi % NX
    y, zl, c = fi // (NLO * 2), (fi // 2) % NLO, fi % 2
    z = zh * NLO + zl

    def at_z(k):
        return (z + k + 2 * NZ) % NZ

    yr, yl = (y + 1) % NY, (y + NY - 1) % NY
    xr, xl = (x + 1) % NX, (x + NX - 1) % NX
    bar = pltpu.get_barrier_semaphore()
    peers = [dev(x, y, z, 1 - c)]
    peers += [dev(x, yn, z, t) for yn in (yr, yl) for t in range(2)]
    peers += [dev(xn, y, z, c) for xn in (xr, xl)]
    peers += [dev(x, y, at_z(s * d), t) for d in range(1, FAR + 1) for s in (1, -1) for t in range(2)]
    for p in peers:
        pl.semaphore_signal(bar, inc=1, device_id=p, device_id_type=MESH)
    loads = [
        pltpu.make_async_copy(ref, own.at[t], loaded.at[t]) for t, ref in enumerate((a_ref, b_ref))
    ]
    for cp in loads:
        cp.start()
    for cp in loads:
        cp.wait()
    xbuf[z, c] = own[c]
    pl.semaphore_wait(bar, len(peers))

    sent = []

    def copy(src, dst, rsem, target):
        cp = pltpu.make_async_remote_copy(
            src_ref=src,
            dst_ref=dst,
            send_sem=ssem.at[len(sent)],
            recv_sem=rsem,
            device_id=target,
            device_id_type=MESH,
        )
        sent.append(cp)
        cp.start()

    def arrived(dst, rsem):
        pltpu.make_async_remote_copy(
            src_ref=dst,
            dst_ref=dst,
            send_sem=ssem.at[0],
            recv_sem=rsem,
            device_id=dev(x, y, z, 1 - c),
            device_id_type=MESH,
        ).wait_recv()

    sign = 1 - 2 * c
    for t in range(2):
        for d in NEXT[0]:
            copy(own.at[t], xbuf.at[z, c], p1r.at[c, d + 5], dev(x, y, at_z(sign * d), t))
        if t == 0:
            pl.semaphore_signal(xin, inc=1, device_id=dev(xl, y, z, c), device_id_type=MESH)
            copy(own.at[1 - c], xbuf.at[z, c], sibr.at[0], dev(x, y, z, 1 - c))
            n_first = 4
            for cp in sent[:n_first]:
                cp.wait_send()
    for n in range(NY // 2 - 1):
        for i, yn in enumerate((yr, yl)):
            pl.semaphore_signal(yin.at[n, i], inc=1, device_id=dev(x, yn, z, c), device_id_type=MESH)
        for i in range(2):
            pl.semaphore_wait(yin.at[n, i], 1)
    pl.semaphore_wait(xin, 1)
    first_view, second_view = own[0].astype(jnp.float32), own[1].astype(jnp.float32)
    dgs[...] = jnp.sum((first_view * second_view).reshape(T // 8, 8, T), axis=0)
    for d in range(1, NX):
        copy(dgs, dgx.at[d - 1], dxr.at[d - 1], dev((x + d) % NX, y, z, c))

    near = jnp.where(zl == 2, 1, NHI - 1)
    group = [zh, (zh + near) % NHI, (zh + NHI - near) % NHI, (zh + 2) % NHI]
    first = jnp.where(zl == 2, T - J, zl * J)
    first = pl.multiple_of(first, 16)

    def send_j():
        xj[:, :, x] = xbuf[pl.ds(zh * NLO, NLO), :, pl.ds(first, J), :]
        for d in (2, 1, 3):
            x1 = (x + d) % NX
            copy(
                xbuf.at[pl.ds(zh * NLO, NLO), :, pl.ds(first, J), :],
                xj.at[:, :, x],
                p2r.at[d - 1],
                dev(x1, y, z, c),
            )

    def wait_j():
        for d in (1, 3, 2):
            arrived(xj.at[:, :, (x + NX - d) % NX], p2r.at[d - 1])

    def gram(k):
        acc = jnp.zeros((JR, T), jnp.float32)
        for i in range(NLO):
            for j in range(2):
                acc += lax.dot_general(
                    xj[i, j].reshape(JR, T),
                    xbuf[group[k] * NLO + i, j],
                    (((1,), (1,)), ((), ())),
                    preferred_element_type=jnp.float32,
                )
        part[k] = acc
        for d in (4, 3, 5, 2, 6, 1, 7):
            y1 = (y + d) % NY
            copy(
                part.at[k, pl.ds(pl.multiple_of(y1 * PY, 8), PY), :],
                rsb.at[k, d - 1],
                rsr.at[k, d - 1],
                dev(x, y1, z, c),
            )

    def reduce(k):
        tot = part[k, pl.ds(pl.multiple_of(y * PY, 8), PY), :]
        for d in (1, 7, 2, 6, 3, 5, 4):
            arrived(rsb.at[k, d - 1], rsr.at[k, d - 1])
            tot += rsb[k, d - 1]
        red[k] = tot
        for d in (4, 3, 5, 2, 6, 1, 7, 0):
            copy(
                red.at[k],
                gt.at[k, pl.ds(pl.multiple_of(y * PY, 8), PY), :],
                agr.at[k, d],
                dev(x, (y + d) % NY, z, 1 - c),
            )

    for d in TREE:
        for j in range(2):
            s = 1 - 2 * j
            zc = at_z(-s * d)
            arrived(xbuf.at[zc, j], p1r.at[j, d + 5])
            for e in NEXT[d]:
                copy(xbuf.at[zc, j], xbuf.at[zc, j], p1r.at[j, e + 5], dev(x, y, at_z(s * (e - d)), c))
        if d == -1:
            arrived(xbuf.at[z, 1 - c], sibr.at[0])
            send_j()
        if d == -3:
            wait_j()
            gram(0)
            gram(1)
        if d == -5:
            gram(2)
    gram(3)
    tot = dgs[...]
    for d in range(1, NX):
        arrived(dgx.at[d - 1], dxr.at[d - 1])
        tot += dgx[d - 1]
    dgs2[...] = tot
    for d in range(1, NHI):
        copy(dgs2, dgz.at[d - 1], dzr.at[d - 1], dev(x, y, (z + NLO * d) % NZ, c))
    for k in range(NHI):
        reduce(k)

    for k in range(NHI):
        for d in range(NY):
            y1 = (y + NY - d) % NY
            arrived(gt.at[k, pl.ds(pl.multiple_of(y1 * PY, 8), PY), :], agr.at[k, d])
        g = gt[k]
        high = g.astype(jnp.bfloat16)
        low = (g - high.astype(jnp.float32)).astype(jnp.bfloat16)
        for d in (1, 2, 0):
            zl1 = (zl + d) % NLO
            for e in range(2):
                tile = xbuf[group[k] * NLO + zl1, e]
                new = jnp.dot(high, tile, preferred_element_type=jnp.float32)
                new += jnp.dot(low, tile, preferred_element_type=jnp.float32)
                new = new.reshape(NX, J, T)
                op[d, :, e] = new if k == 0 else op[d, :, e] + new
            if k == NHI - 1:
                for i in (2, 1, 3):
                    x1 = (x + i) % NX
                    copy(op.at[d, x1], rx.at[d, i - 1], p4r.at[d, i - 1], dev(x1, y, z, c))
    for d in (1, 2, 0):
        zl1 = (zl + d) % NLO
        total = op[d, x]
        for i in (1, 3, 2):
            arrived(rx.at[d, i - 1], p4r.at[d, i - 1])
            total += rx[d, i - 1]
        fsum[d] = total
        for e in range(2):
            c1 = (c + e) % 2
            if d or e:
                copy(fsum.at[d, c1], fin.at[c, zl], p5r.at[d, e], dev(x, y, zh * NLO + zl1, c1))
            else:
                fin[c, zl] = fsum[d, c]
    hops = [(d, e) for d in (0, 1, 2) for e in range(2) if d or e]
    tot = dgs2[...]
    for d in range(1, NHI):
        arrived(dgz.at[d - 1], dzr.at[d - 1])
        tot += dgz[d - 1]
    weight_off = w_ref[0]
    shift = -2.0 + (2.0 * (1.0 - weight_off) / images) * jnp.sum(tot, axis=0, keepdims=True)
    scale = 2.0 * weight_off / images
    for d, e in hops:
        arrived(fin.at[(c + e) % 2, (zl + NLO - d) % NLO], p5r.at[d, e])
    for t in range(2):
        other = own.at[1 - t]
        for i, rows in enumerate((J, J, T - 2 * J)):
            at = pl.ds(i * J, rows)
            gram_term = fin[t, i, pl.ds(J - rows, rows), :]
            g_ref[t, at, :] = scale * gram_term + other[at, :].astype(jnp.float32) * shift
    for cp in sent[n_first:]:
        cp.wait_send()


def local(view_a, view_b, weight_off, loss_grad):
    images = view_a.shape[0] * lax.axis_size("batch")
    f32, bf16 = jnp.float32, jnp.bfloat16
    dma = pltpu.SemaphoreType.DMA
    vmem = pl.BlockSpec(memory_space=pltpu.VMEM)
    hbm = pl.BlockSpec(memory_space=pl.ANY)
    smem = pl.BlockSpec(memory_space=pltpu.SMEM)
    grads = pl.pallas_call(
        functools.partial(kernel, float(images)),
        out_shape=jax.ShapeDtypeStruct((2, T, T), f32),
        in_specs=[smem, hbm, hbm],
        out_specs=vmem,
        scratch_shapes=[
            pltpu.VMEM((2, T, T), bf16),
            pltpu.VMEM((NZ, 2, T, T), bf16),
            pltpu.VMEM((NLO, 2, NX, J, T), bf16),
            pltpu.VMEM((NHI, JR, T), f32),
            pltpu.VMEM((NHI, NY - 1, PY, T), f32),
            pltpu.VMEM((NHI, PY, T), f32),
            pltpu.VMEM((NHI, JR, T), f32),
            pltpu.VMEM((NLO, NX, 2, J, T), f32),
            pltpu.VMEM((NLO, NX - 1, 2, J, T), f32),
            pltpu.VMEM((NLO, 2, J, T), f32),
            pltpu.VMEM((2, NLO, J, T), f32),
            pltpu.VMEM((8, T), f32),
            pltpu.VMEM((NX - 1, 8, T), f32),
            pltpu.VMEM((8, T), f32),
            pltpu.VMEM((NHI - 1, 8, T), f32),
            dma((112,)),
            dma((2,)),
            pltpu.SemaphoreType.REGULAR,
            pltpu.SemaphoreType.REGULAR((NY // 2 - 1, 2)),
            dma((2, 12)),
            dma((1,)),
            dma((NX - 1,)),
            dma((NHI, NY - 1)),
            dma((NHI, NY)),
            dma((NLO, NX - 1)),
            dma((NLO, 2)),
            dma((NX - 1,)),
            dma((NHI - 1,)),
        ],
        compiler_params=pltpu.CompilerParams(
            collective_id=0, has_side_effects=True, vmem_limit_bytes=60 << 20
        ),
        name="gram_grads",
    )(weight_off.reshape(1), view_a, view_b)
    return loss_grad * grads[0], loss_grad * grads[1]


def solution(mesh):
    return jax.shard_map(
        local,
        mesh=mesh,
        in_specs=(P("batch", "feat"), P("batch", "feat"), P(), P()),
        out_specs=(P("batch", "feat"), P("batch", "feat")),
        check_vma=False,
    )
```

```python
import functools

import jax
import jax.numpy as jnp
from jax import lax
from jax.experimental import pallas as pl
from jax.experimental.pallas import tpu as pltpu
from jax.sharding import PartitionSpec as P

MESH = pl.DeviceIdType.MESH
NX, NY, NHI, NLO = 4, 8, 4, 3
NZ = NHI * NLO
T = 128
J = 48
JR = NX * J
PY = JR // NY
TREE = {1: 0, -1: 0, 2: 1, -2: -1, 3: 2, -3: -2, 4: 3, -4: -3, 5: 4, -5: -4, 6: 5}
NEXT = {p: [d for d in TREE if TREE[d] == p] for p in (0, *TREE)}
FAR = max(abs(d) for d in NEXT[0])


def dev(x, y, z, c):
    return ((z // NLO) * NX + x, (y * NLO + z % NLO) * 2 + c)


def kernel(
    images,
    w_ref,
    own,
    g_ref,
    xbuf,
    xj,
    part,
    rsb,
    red,
    gt,
    op,
    rx,
    fsum,
    fin,
    dgs,
    dgx,
    dgs2,
    dgz,
    ssem,
    xin,
    yin,
    p1r,
    sibr,
    p2r,
    rsr,
    agr,
    p4r,
    p5r,
    dxr,
    dzr,
):
    bi = lax.axis_index("batch")
    fi = lax.axis_index("feat")
    zh, x = bi // NX, bi % NX
    y, zl, c = fi // (NLO * 2), (fi // 2) % NLO, fi % 2
    z = zh * NLO + zl

    def at_z(k):
        return (z + k + 2 * NZ) % NZ

    yr, yl = (y + 1) % NY, (y + NY - 1) % NY
    xr, xl = (x + 1) % NX, (x + NX - 1) % NX
    bar = pltpu.get_barrier_semaphore()
    peers = [dev(x, y, z, 1 - c)]
    peers += [dev(x, yn, z, t) for yn in (yr, yl) for t in range(2)]
    peers += [dev(xn, y, z, c) for xn in (xr, xl)]
    peers += [dev(x, y, at_z(s * d), t) for d in range(1, FAR + 1) for s in (1, -1) for t in range(2)]
    for p in peers:
        pl.semaphore_signal(bar, inc=1, device_id=p, device_id_type=MESH)
    xbuf[z, c] = own[c]
    pl.semaphore_wait(bar, len(peers))

    sent = []

    def copy(src, dst, rsem, target):
        cp = pltpu.make_async_remote_copy(
            src_ref=src,
            dst_ref=dst,
            send_sem=ssem.at[len(sent)],
            recv_sem=rsem,
            device_id=target,
            device_id_type=MESH,
        )
        sent.append(cp)
        cp.start()

    def arrived(dst, rsem):
        pltpu.make_async_remote_copy(
            src_ref=dst,
            dst_ref=dst,
            send_sem=ssem.at[0],
            recv_sem=rsem,
            device_id=dev(x, y, z, 1 - c),
            device_id_type=MESH,
        ).wait_recv()

    sign = 1 - 2 * c
    for t in range(2):
        for d in NEXT[0]:
            copy(own.at[t], xbuf.at[z, c], p1r.at[c, d + 5], dev(x, y, at_z(sign * d), t))
        if t == 0:
            pl.semaphore_signal(xin, inc=1, device_id=dev(xl, y, z, c), device_id_type=MESH)
            copy(own.at[1 - c], xbuf.at[z, c], sibr.at[0], dev(x, y, z, 1 - c))
    for n in range(NY // 2 - 1):
        for i, yn in enumerate((yr, yl)):
            pl.semaphore_signal(yin.at[n, i], inc=1, device_id=dev(x, yn, z, c), device_id_type=MESH)
        for i in range(2):
            pl.semaphore_wait(yin.at[n, i], 1)
    pl.semaphore_wait(xin, 1)
    first_view, second_view = own[0].astype(jnp.float32), own[1].astype(jnp.float32)
    dgs[...] = jnp.sum((first_view * second_view).reshape(T // 8, 8, T), axis=0)
    for d in range(1, NX):
        copy(dgs, dgx.at[d - 1], dxr.at[d - 1], dev((x + d) % NX, y, z, c))

    near = jnp.where(zl == 2, 1, NHI - 1)
    group = [zh, (zh + near) % NHI, (zh + NHI - near) % NHI, (zh + 2) % NHI]
    first = jnp.where(zl == 2, T - J, zl * J)
    first = pl.multiple_of(first, 16)

    def send_j():
        xj[:, :, x] = xbuf[pl.ds(zh * NLO, NLO), :, pl.ds(first, J), :]
        for d in (2, 1, 3):
            x1 = (x + d) % NX
            copy(
                xbuf.at[pl.ds(zh * NLO, NLO), :, pl.ds(first, J), :],
                xj.at[:, :, x],
                p2r.at[d - 1],
                dev(x1, y, z, c),
            )

    def wait_j():
        for d in (1, 3, 2):
            arrived(xj.at[:, :, (x + NX - d) % NX], p2r.at[d - 1])

    def gram(k):
        acc = jnp.zeros((JR, T), jnp.float32)
        for i in range(NLO):
            for j in range(2):
                acc += lax.dot_general(
                    xj[i, j].reshape(JR, T),
                    xbuf[group[k] * NLO + i, j],
                    (((1,), (1,)), ((), ())),
                    preferred_element_type=jnp.float32,
                )
        part[k] = acc
        for d in (4, 3, 5, 2, 6, 1, 7):
            y1 = (y + d) % NY
            copy(
                part.at[k, pl.ds(pl.multiple_of(y1 * PY, 8), PY), :],
                rsb.at[k, d - 1],
                rsr.at[k, d - 1],
                dev(x, y1, z, c),
            )

    def reduce(k):
        tot = part[k, pl.ds(pl.multiple_of(y * PY, 8), PY), :]
        for d in (1, 7, 2, 6, 3, 5, 4):
            arrived(rsb.at[k, d - 1], rsr.at[k, d - 1])
            tot += rsb[k, d - 1]
        red[k] = tot
        for d in (4, 3, 5, 2, 6, 1, 7, 0):
            copy(
                red.at[k],
                gt.at[k, pl.ds(pl.multiple_of(y * PY, 8), PY), :],
                agr.at[k, d],
                dev(x, (y + d) % NY, z, 1 - c),
            )

    for d in TREE:
        for j in range(2):
            s = 1 - 2 * j
            zc = at_z(-s * d)
            arrived(xbuf.at[zc, j], p1r.at[j, d + 5])
            for e in NEXT[d]:
                copy(xbuf.at[zc, j], xbuf.at[zc, j], p1r.at[j, e + 5], dev(x, y, at_z(s * (e - d)), c))
        if d == -1:
            arrived(xbuf.at[z, 1 - c], sibr.at[0])
        if d == -2:
            send_j()
        if d == -3:
            wait_j()
            gram(0)
        if d == -4:
            gram(1)
        if d == -5:
            gram(2)
    gram(3)
    tot = dgs[...]
    for d in range(1, NX):
        arrived(dgx.at[d - 1], dxr.at[d - 1])
        tot += dgx[d - 1]
    dgs2[...] = tot
    for d in range(1, NHI):
        copy(dgs2, dgz.at[d - 1], dzr.at[d - 1], dev(x, y, (z + NLO * d) % NZ, c))
    for k in range(NHI):
        reduce(k)

    for k in range(NHI):
        for d in range(NY):
            y1 = (y + NY - d) % NY
            arrived(gt.at[k, pl.ds(pl.multiple_of(y1 * PY, 8), PY), :], agr.at[k, d])
        g = gt[k]
        high = g.astype(jnp.bfloat16)
        low = (g - high.astype(jnp.float32)).astype(jnp.bfloat16)
        for d in (1, 2, 0):
            zl1 = (zl + d) % NLO
            for e in range(2):
                tile = xbuf[group[k] * NLO + zl1, e]
                new = jnp.dot(high, tile, preferred_element_type=jnp.float32)
                new += jnp.dot(low, tile, preferred_element_type=jnp.float32)
                new = new.reshape(NX, J, T)
                op[d, :, e] = new if k == 0 else op[d, :, e] + new
            if k == NHI - 1:
                for i in (2, 1, 3):
                    x1 = (x + i) % NX
                    copy(op.at[d, x1], rx.at[d, i - 1], p4r.at[d, i - 1], dev(x1, y, z, c))
    for d in (1, 2, 0):
        zl1 = (zl + d) % NLO
        total = op[d, x]
        for i in (1, 3, 2):
            arrived(rx.at[d, i - 1], p4r.at[d, i - 1])
            total += rx[d, i - 1]
        fsum[d] = total
        for e in range(2):
            c1 = (c + e) % 2
            if d or e:
                copy(fsum.at[d, c1], fin.at[c, zl], p5r.at[d, e], dev(x, y, zh * NLO + zl1, c1))
            else:
                fin[c, zl] = fsum[d, c]
    hops = [(d, e) for d in (0, 1, 2) for e in range(2) if d or e]
    tot = dgs2[...]
    for d in range(1, NHI):
        arrived(dgz.at[d - 1], dzr.at[d - 1])
        tot += dgz[d - 1]
    weight_off = w_ref[0]
    shift = -2.0 + (2.0 * (1.0 - weight_off) / images) * jnp.sum(tot, axis=0, keepdims=True)
    scale = 2.0 * weight_off / images
    for d, e in hops:
        arrived(fin.at[(c + e) % 2, (zl + NLO - d) % NLO], p5r.at[d, e])
    for t in range(2):
        other = own.at[1 - t]
        for i, rows in enumerate((J, J, T - 2 * J)):
            at = pl.ds(i * J, rows)
            gram_term = fin[t, i, pl.ds(J - rows, rows), :]
            g_ref[t, at, :] = scale * gram_term + other[at, :].astype(jnp.float32) * shift
    for cp in sent:
        cp.wait_send()


def local(view_a, view_b, weight_off, loss_grad):
    images = view_a.shape[0] * lax.axis_size("batch")
    f32, bf16 = jnp.float32, jnp.bfloat16
    dma = pltpu.SemaphoreType.DMA
    vmem = pl.BlockSpec(memory_space=pltpu.VMEM)
    smem = pl.BlockSpec(memory_space=pltpu.SMEM)
    grads = pl.pallas_call(
        functools.partial(kernel, float(images)),
        out_shape=jax.ShapeDtypeStruct((2, T, T), f32),
        in_specs=[smem, vmem],
        out_specs=vmem,
        scratch_shapes=[
            pltpu.VMEM((NZ, 2, T, T), bf16),
            pltpu.VMEM((NLO, 2, NX, J, T), bf16),
            pltpu.VMEM((NHI, JR, T), f32),
            pltpu.VMEM((NHI, NY - 1, PY, T), f32),
            pltpu.VMEM((NHI, PY, T), f32),
            pltpu.VMEM((NHI, JR, T), f32),
            pltpu.VMEM((NLO, NX, 2, J, T), f32),
            pltpu.VMEM((NLO, NX - 1, 2, J, T), f32),
            pltpu.VMEM((NLO, 2, J, T), f32),
            pltpu.VMEM((2, NLO, J, T), f32),
            pltpu.VMEM((8, T), f32),
            pltpu.VMEM((NX - 1, 8, T), f32),
            pltpu.VMEM((8, T), f32),
            pltpu.VMEM((NHI - 1, 8, T), f32),
            dma((112,)),
            pltpu.SemaphoreType.REGULAR,
            pltpu.SemaphoreType.REGULAR((NY // 2 - 1, 2)),
            dma((2, 12)),
            dma((1,)),
            dma((NX - 1,)),
            dma((NHI, NY - 1)),
            dma((NHI, NY)),
            dma((NLO, NX - 1)),
            dma((NLO, 2)),
            dma((NX - 1,)),
            dma((NHI - 1,)),
        ],
        compiler_params=pltpu.CompilerParams(
            collective_id=0, has_side_effects=True, vmem_limit_bytes=32 << 20
        ),
        name="gram_grads",
    )(weight_off.reshape(1), jnp.stack([view_a, view_b]))
    return loss_grad * grads[0], loss_grad * grads[1]


def solution(mesh):
    return jax.shard_map(
        local,
        mesh=mesh,
        in_specs=(P("batch", "feat"), P("batch", "feat"), P(), P()),
        out_specs=(P("batch", "feat"), P("batch", "feat")),
        check_vma=False,
    )
```

```python
import functools

import jax
import jax.numpy as jnp
from jax import lax
from jax.experimental import pallas as pl
from jax.experimental.pallas import tpu as pltpu
from jax.sharding import PartitionSpec as P

MESH = pl.DeviceIdType.MESH
NX, NY, NHI, NLO = 4, 8, 4, 3
NZ = NHI * NLO
T = 128
J = 48
JR = NX * J
PY = JR // NY
TREE = {1: 0, -1: 0, 2: 1, -2: -1, 3: 2, -3: -2, 4: 3, -4: -3, 5: 4, -5: -4, 6: 5}
NEXT = {p: [d for d in TREE if TREE[d] == p] for p in (0, *TREE)}
FAR = max(abs(d) for d in NEXT[0])


def dev(x, y, z, c):
    return ((z // NLO) * NX + x, (y * NLO + z % NLO) * 2 + c)


def kernel(
    images,
    w_ref,
    own,
    g_ref,
    xbuf,
    xj,
    part,
    rsb,
    red,
    gt,
    op,
    rx,
    fsum,
    fin,
    dgs,
    dgx,
    dgs2,
    dgz,
    ssem,
    xin,
    yin,
    p1r,
    sibr,
    p2r,
    rsr,
    agr,
    p4r,
    p5r,
    dxr,
    dzr,
):
    bi = lax.axis_index("batch")
    fi = lax.axis_index("feat")
    zh, x = bi // NX, bi % NX
    y, zl, c = fi // (NLO * 2), (fi // 2) % NLO, fi % 2
    z = zh * NLO + zl

    def at_z(k):
        return (z + k + 2 * NZ) % NZ

    yr, yl = (y + 1) % NY, (y + NY - 1) % NY
    xr, xl = (x + 1) % NX, (x + NX - 1) % NX
    bar = pltpu.get_barrier_semaphore()
    peers = [dev(x, y, z, 1 - c)]
    peers += [dev(x, yn, z, t) for yn in (yr, yl) for t in range(2)]
    peers += [dev(xn, y, z, c) for xn in (xr, xl)]
    peers += [dev(x, y, at_z(s * d), t) for d in range(1, FAR + 1) for s in (1, -1) for t in range(2)]
    for p in peers:
        pl.semaphore_signal(bar, inc=1, device_id=p, device_id_type=MESH)
    xbuf[z, c] = own[c]
    pl.semaphore_wait(bar, len(peers))

    sent = []

    def copy(src, dst, rsem, target):
        cp = pltpu.make_async_remote_copy(
            src_ref=src,
            dst_ref=dst,
            send_sem=ssem.at[len(sent)],
            recv_sem=rsem,
            device_id=target,
            device_id_type=MESH,
        )
        sent.append(cp)
        cp.start()

    def arrived(dst, rsem):
        pltpu.make_async_remote_copy(
            src_ref=dst,
            dst_ref=dst,
            send_sem=ssem.at[0],
            recv_sem=rsem,
            device_id=dev(x, y, z, 1 - c),
            device_id_type=MESH,
        ).wait_recv()

    sign = 1 - 2 * c
    for t in range(2):
        for d in NEXT[0]:
            copy(own.at[t], xbuf.at[z, c], p1r.at[c, d + 5], dev(x, y, at_z(sign * d), t))
        if t == 0:
            pl.semaphore_signal(xin, inc=1, device_id=dev(xl, y, z, c), device_id_type=MESH)
            copy(own.at[1 - c], xbuf.at[z, c], sibr.at[0], dev(x, y, z, 1 - c))
    for n in range(NY // 2 - 1):
        for i, yn in enumerate((yr, yl)):
            pl.semaphore_signal(yin.at[n, i], inc=1, device_id=dev(x, yn, z, c), device_id_type=MESH)
        for i in range(2):
            pl.semaphore_wait(yin.at[n, i], 1)
    pl.semaphore_wait(xin, 1)
    first_view, second_view = own[0].astype(jnp.float32), own[1].astype(jnp.float32)
    dgs[...] = jnp.sum((first_view * second_view).reshape(T // 8, 8, T), axis=0)
    for d in range(1, NX):
        copy(dgs, dgx.at[d - 1], dxr.at[d - 1], dev((x + d) % NX, y, z, c))

    near = jnp.where(zl == 2, 1, NHI - 1)
    group = [zh, (zh + near) % NHI, (zh + NHI - near) % NHI, (zh + 2) % NHI]
    first = jnp.where(zl == 2, T - J, zl * J)
    first = pl.multiple_of(first, 16)

    def send_j():
        xj[:, :, x] = xbuf[pl.ds(zh * NLO, NLO), :, pl.ds(first, J), :]
        for d in (2, 1, 3):
            x1 = (x + d) % NX
            copy(
                xbuf.at[pl.ds(zh * NLO, NLO), :, pl.ds(first, J), :],
                xj.at[:, :, x],
                p2r.at[d - 1],
                dev(x1, y, z, c),
            )

    def wait_j():
        for d in (1, 3, 2):
            arrived(xj.at[:, :, (x + NX - d) % NX], p2r.at[d - 1])

    def gram(k):
        acc = jnp.zeros((JR, T), jnp.float32)
        for i in range(NLO):
            for j in range(2):
                acc += lax.dot_general(
                    xj[i, j].reshape(JR, T),
                    xbuf[group[k] * NLO + i, j],
                    (((1,), (1,)), ((), ())),
                    preferred_element_type=jnp.float32,
                )
        part[k] = acc
        for d in (4, 3, 5, 2, 6, 1, 7):
            y1 = (y + d) % NY
            copy(
                part.at[k, pl.ds(pl.multiple_of(y1 * PY, 8), PY), :],
                rsb.at[k, d - 1],
                rsr.at[k, d - 1],
                dev(x, y1, z, c),
            )

    def reduce(k):
        tot = part[k, pl.ds(pl.multiple_of(y * PY, 8), PY), :]
        for d in (1, 7, 2, 6, 3, 5, 4):
            arrived(rsb.at[k, d - 1], rsr.at[k, d - 1])
            tot += rsb[k, d - 1]
        red[k] = tot
        for d in (4, 3, 5, 2, 6, 1, 7, 0):
            copy(
                red.at[k],
                gt.at[k, pl.ds(pl.multiple_of(y * PY, 8), PY), :],
                agr.at[k, d],
                dev(x, (y + d) % NY, z, 1 - c),
            )

    for d in TREE:
        for j in range(2):
            s = 1 - 2 * j
            zc = at_z(-s * d)
            arrived(xbuf.at[zc, j], p1r.at[j, d + 5])
            for e in NEXT[d]:
                copy(xbuf.at[zc, j], xbuf.at[zc, j], p1r.at[j, e + 5], dev(x, y, at_z(s * (e - d)), c))
        if d == -1:
            arrived(xbuf.at[z, 1 - c], sibr.at[0])
        if d == -2:
            send_j()
        if d == -3:
            wait_j()
            gram(0)
        if d == -4:
            gram(1)
        if d == -5:
            gram(2)
    gram(3)
    for k in range(NHI):
        reduce(k)

    tot = dgs[...]
    for d in range(1, NX):
        arrived(dgx.at[d - 1], dxr.at[d - 1])
        tot += dgx[d - 1]
    dgs2[...] = tot
    for d in range(1, NHI):
        copy(dgs2, dgz.at[d - 1], dzr.at[d - 1], dev(x, y, (z + NLO * d) % NZ, c))
    for k in range(NHI):
        for d in range(NY):
            y1 = (y + NY - d) % NY
            arrived(gt.at[k, pl.ds(pl.multiple_of(y1 * PY, 8), PY), :], agr.at[k, d])
        g = gt[k]
        high = g.astype(jnp.bfloat16)
        low = (g - high.astype(jnp.float32)).astype(jnp.bfloat16)
        for d in (1, 2, 0):
            zl1 = (zl + d) % NLO
            for e in range(2):
                tile = xbuf[group[k] * NLO + zl1, e]
                new = jnp.dot(high, tile, preferred_element_type=jnp.float32)
                new += jnp.dot(low, tile, preferred_element_type=jnp.float32)
                new = new.reshape(NX, J, T)
                op[d, :, e] = new if k == 0 else op[d, :, e] + new
            if k == NHI - 1:
                for i in (2, 1, 3):
                    x1 = (x + i) % NX
                    copy(op.at[d, x1], rx.at[d, i - 1], p4r.at[d, i - 1], dev(x1, y, z, c))
    for d in (1, 2, 0):
        zl1 = (zl + d) % NLO
        total = op[d, x]
        for i in (1, 3, 2):
            arrived(rx.at[d, i - 1], p4r.at[d, i - 1])
            total += rx[d, i - 1]
        fsum[d] = total
        for e in range(2):
            c1 = (c + e) % 2
            if d or e:
                copy(fsum.at[d, c1], fin.at[c, zl], p5r.at[d, e], dev(x, y, zh * NLO + zl1, c1))
            else:
                fin[c, zl] = fsum[d, c]
    hops = [(d, e) for d in (0, 1, 2) for e in range(2) if d or e]
    tot = dgs2[...]
    for d in range(1, NHI):
        arrived(dgz.at[d - 1], dzr.at[d - 1])
        tot += dgz[d - 1]
    weight_off = w_ref[0]
    shift = -2.0 + (2.0 * (1.0 - weight_off) / images) * jnp.sum(tot, axis=0, keepdims=True)
    scale = 2.0 * weight_off / images
    for d, e in hops:
        arrived(fin.at[(c + e) % 2, (zl + NLO - d) % NLO], p5r.at[d, e])
    for t in range(2):
        other = own.at[1 - t]
        for i, rows in enumerate((J, J, T - 2 * J)):
            at = pl.ds(i * J, rows)
            gram_term = fin[t, i, pl.ds(J - rows, rows), :]
            g_ref[t, at, :] = scale * gram_term + other[at, :].astype(jnp.float32) * shift
    for cp in sent:
        cp.wait_send()


def local(view_a, view_b, weight_off, loss_grad):
    images = view_a.shape[0] * lax.axis_size("batch")
    f32, bf16 = jnp.float32, jnp.bfloat16
    dma = pltpu.SemaphoreType.DMA
    vmem = pl.BlockSpec(memory_space=pltpu.VMEM)
    smem = pl.BlockSpec(memory_space=pltpu.SMEM)
    grads = pl.pallas_call(
        functools.partial(kernel, float(images)),
        out_shape=jax.ShapeDtypeStruct((2, T, T), f32),
        in_specs=[smem, vmem],
        out_specs=vmem,
        scratch_shapes=[
            pltpu.VMEM((NZ, 2, T, T), bf16),
            pltpu.VMEM((NLO, 2, NX, J, T), bf16),
            pltpu.VMEM((NHI, JR, T), f32),
            pltpu.VMEM((NHI, NY - 1, PY, T), f32),
            pltpu.VMEM((NHI, PY, T), f32),
            pltpu.VMEM((NHI, JR, T), f32),
            pltpu.VMEM((NLO, NX, 2, J, T), f32),
            pltpu.VMEM((NLO, NX - 1, 2, J, T), f32),
            pltpu.VMEM((NLO, 2, J, T), f32),
            pltpu.VMEM((2, NLO, J, T), f32),
            pltpu.VMEM((8, T), f32),
            pltpu.VMEM((NX - 1, 8, T), f32),
            pltpu.VMEM((8, T), f32),
            pltpu.VMEM((NHI - 1, 8, T), f32),
            dma((112,)),
            pltpu.SemaphoreType.REGULAR,
            pltpu.SemaphoreType.REGULAR((NY // 2 - 1, 2)),
            dma((2, 12)),
            dma((1,)),
            dma((NX - 1,)),
            dma((NHI, NY - 1)),
            dma((NHI, NY)),
            dma((NLO, NX - 1)),
            dma((NLO, 2)),
            dma((NX - 1,)),
            dma((NHI - 1,)),
        ],
        compiler_params=pltpu.CompilerParams(
            collective_id=0, has_side_effects=True, vmem_limit_bytes=32 << 20
        ),
        name="gram_grads",
    )(weight_off.reshape(1), jnp.stack([view_a, view_b]))
    return loss_grad * grads[0], loss_grad * grads[1]


def solution(mesh):
    return jax.shard_map(
        local,
        mesh=mesh,
        in_specs=(P("batch", "feat"), P("batch", "feat"), P(), P()),
        out_specs=(P("batch", "feat"), P("batch", "feat")),
        check_vma=False,
    )
```
